32 devices in a mesh: seq: 16 (over z, y, x), head: 2 (over core).
Axes of the slice: x: 2, y: 2, z: 4, core: 2. Of those that a mesh axis runs over, the one named last changes fastest.
Arguments:
- tokens: float32 [2, 4096, 768], P(None, 'seq'), may hold values from -6 to 6
- norm_gain: float32 [768], replicated, may hold values from 0.5 to 1.5
- w_gate: float32 [768, 1536], P(None, 'head'), may hold values from -0.21875 to 0.21875
- w_inner: float32 [768, 1536], P(None, 'head'), may hold values from -0.21875 to 0.21875
- w_state: float32 [768, 256], replicated, may hold values from -0.21875 to 0.21875
- w_step: float32 [768, 24], P(None, 'head'), may hold values from -0.21875 to 0.21875
- conv_inner: float32 [4, 1536], P(None, 'head'), may hold values from -3 to 3
- conv_state: float32 [4, 256], replicated, may hold values from -3 to 3
- bias_inner: float32 [1536], P('head'), may hold values from -3 to 3
- bias_state: float32 [256], replicated, may hold values from -3 to 3
- step_bias: float32 [24], P('head'), may hold values from -4 to -2
- decay_log: float32 [24], P('head'), may hold values from -7.5 to 0
- skip_gain: float32 [24], P('head'), may hold values from 0.5 to 1.5
- out_gain: float32 [1536], P('head'), may hold values from 0.5 to 1.5
- w_out: float32 [1536, 768], P('head'), may hold values from -0.15625 to 0.15625
- cotangent: float32 [2, 4096, 768], P(None, 'seq', 'head'), may hold values from -6 to 6
Outputs:
- result: float32 [2, 4096, 768], P(None, 'seq', 'head')
- grad_tokens: float32 [2, 4096, 768], P(None, 'seq', 'head')
- grad_norm_gain: float32 [768], replicated
- grad_w_gate: float32 [768, 1536], P(None, 'head')
- grad_w_inner: float32 [768, 1536], P(None, 'head')
- grad_w_state: float32 [768, 256], replicated
- grad_w_step: float32 [768, 24], P(None, 'head')
- grad_conv_inner: float32 [4, 1536], P(None, 'head')
- grad_conv_state: float32 [4, 256], replicated
- grad_bias_inner: float32 [1536], P('head')
- grad_bias_state: float32 [256], replicated
- grad_step_bias: float32 [24], P('head')
- grad_decay_log: float32 [24], P('head')
- grad_skip_gain: float32 [24], P('head')
- grad_out_gain: float32 [1536], P('head')
- grad_w_out: float32 [1536, 768], P('head')
The draws below stay inside these ranges and needn't reach their ends.
All inputs are finite; a program needn't handle non-finite values.
Results may differ from the reference program's by a relative error of at most 0.0003.
Values sent between devices are 32-bit elements; how exact they have to be, the bound alone decides.
A program may use at most 256 MiB of HBM per device.

```python
import jax
import jax.numpy as jnp
from jax import lax

D = 768
HEADS = 24
HEAD_DIM = 64
STATE = 128
CONV = 4
GROUP = 256
SEQS = 2
INNER = 1536
LEN = 4096


def block_scale(stream_key, dims, shards, smallest, top_value):
    def one(dim, blocks):
        draws = jax.random.uniform(jax.random.fold_in(jax.random.fold_in(stream_key, 6), dim), (blocks,), jnp.float32, smallest / len(shards), top_value / len(shards))
        return jnp.repeat(jnp.exp(draws), dims[dim] // blocks).reshape((-1,) + (1,) * (len(dims) - dim - 1))

    factor_of = one(*shards[0])
    for cut in shards[1:]:
        factor_of = factor_of * one(*cut)
    return factor_of


def scatter_about(stream_key, shape, width, reach, pieces=(), kind=jnp.bfloat16):
    result = width * jax.random.normal(stream_key, shape, jnp.float32)
    if pieces:
        result = result * block_scale(stream_key, shape, pieces, -0.22, 0.18)
    return jnp.clip(result, -reach, reach).astype(kind)


def setup_inputs(seed: int = 0) -> dict:
    arg_keys = jax.random.split(jax.random.key(seed), 17)
    tokens = scatter_about(arg_keys[0], (SEQS, LEN, D), 1.0, 6.0, ((1, 16),), jnp.float32)
    norm_gain = jnp.clip(1.0 + 0.1 * jax.random.normal(arg_keys[1], (D,), jnp.float32), 0.5, 1.5)
    w_gate = scatter_about(arg_keys[2], (D, INNER), D ** -0.5, 0.21875, ((1, 2),), jnp.float32)
    w_inner = scatter_about(arg_keys[3], (D, INNER), D ** -0.5, 0.21875, ((1, 2),), jnp.float32)
    w_state = scatter_about(arg_keys[4], (D, 2 * STATE), D ** -0.5, 0.21875, (), jnp.float32)
    w_step = scatter_about(arg_keys[5], (D, HEADS), D ** -0.5, 0.21875, ((1, 2),), jnp.float32)
    conv_inner = scatter_about(arg_keys[6], (CONV, INNER), 0.5, 3.0, ((1, 2),), jnp.float32)
    conv_state = scatter_about(arg_keys[7], (CONV, 2 * STATE), 0.5, 3.0, (), jnp.float32)
    bias_inner = scatter_about(arg_keys[8], (INNER,), 0.5, 3.0, ((0, 2),), jnp.float32)
    bias_state = scatter_about(arg_keys[9], (2 * STATE,), 0.5, 3.0, (), jnp.float32)
    step_bias = jnp.clip(-4.0 + 2.0 * jax.random.uniform(arg_keys[10], (HEADS,), jnp.float32) ** block_scale(arg_keys[10], (HEADS,), ((0, 2),), -0.2, 0.2), -4.0, -2.0)
    decay_log = jnp.clip(-7.5 + 7.5 * jax.random.uniform(arg_keys[11], (HEADS,), jnp.float32) ** block_scale(arg_keys[11], (HEADS,), ((0, 2),), -0.2, 0.2), -7.5, 0.0)
    skip_gain = jnp.clip(0.5 + 1.0 * jax.random.uniform(arg_keys[12], (HEADS,), jnp.float32) ** block_scale(arg_keys[12], (HEADS,), ((0, 2),), -0.2, 0.2), 0.5, 1.5)
    out_gain = jnp.clip(1.0 + 0.1 * jax.random.normal(arg_keys[13], (INNER,), jnp.float32), 0.5, 1.5)
    w_out = scatter_about(arg_keys[14], (INNER, D), INNER ** -0.5, 0.15625, ((0, 2),), jnp.float32)
    cotangent = scatter_about(arg_keys[15], (SEQS, LEN, D), 1.0, 6.0, ((1, 16), (2, 2)), jnp.float32)
    return dict(tokens=tokens, norm_gain=norm_gain, w_gate=w_gate, w_inner=w_inner, w_state=w_state, w_step=w_step, conv_inner=conv_inner, conv_state=conv_state, bias_inner=bias_inner, bias_state=bias_state, step_bias=step_bias, decay_log=decay_log, skip_gain=skip_gain, out_gain=out_gain, w_out=w_out, cotangent=cotangent)


highest = lax.Precision.HIGHEST
epsilon = 1e-05

@jax.custom_vjp
def low(v):
    return lax.optimization_barrier(v.astype(jnp.bfloat16)).astype(jnp.float32)

@jax.custom_vjp
def low_back(v):
    return v

def low_keep(v):
    return (low(v), None)

def low_pass(kept, grad):
    return (grad,)

def back_keep(v):
    return (v, None)

def back_low(kept, grad):
    return (low(grad),)
low.defvjp(low_keep, low_pass)
low_back.defvjp(back_keep, back_low)

def mamba_layer(tokens, norm_gain, w_gate, w_inner, w_state, w_step, conv_inner, conv_state, bias_inner, bias_state, step_bias, decay_log, skip_gain, out_gain, w_out):
    length = tokens.shape[0]
    hidden = tokens * lax.rsqrt(lax.optimization_barrier(jnp.mean(tokens * tokens, axis=-1, keepdims=True)) + epsilon) * norm_gain
    gate_proj = jnp.dot(hidden, w_gate, precision=highest)
    mixed_in = jnp.concatenate([jnp.dot(hidden, w_inner, precision=highest), jnp.dot(hidden, w_state, precision=highest)], axis=-1)
    raw_step = jnp.dot(hidden, w_step, precision=highest)
    weights = jnp.concatenate([conv_inner, conv_state], axis=-1)
    summed = jnp.concatenate([bias_inner, bias_state], axis=-1) + jnp.zeros_like(mixed_in)
    padded = jnp.concatenate([jnp.zeros((CONV - 1, mixed_in.shape[1]), jnp.float32), mixed_in], axis=0)
    for offset in range(CONV):
        summed = summed + weights[offset] * padded[offset:offset + length]
    active = jax.nn.silu(summed)
    step_size = jax.nn.softplus(raw_step + step_bias)
    rate = -jnp.exp(decay_log) * step_size
    groups = length // GROUP
    blocks = (active[:, :INNER].reshape(groups, GROUP, HEADS, HEAD_DIM), active[:, INNER:INNER + STATE].reshape(groups, GROUP, STATE), active[:, INNER + STATE:].reshape(groups, GROUP, STATE), step_size.reshape(groups, GROUP, HEADS), rate.reshape(groups, GROUP, HEADS))
    causal = jnp.arange(GROUP)[:, None] >= jnp.arange(GROUP)[None, :]

    def group_step(entering, group_data):
        inner_x, input_map, output_map, step_here, rate_here = group_data
        cumulative = jnp.cumsum(rate_here, axis=0)
        scores = jnp.dot(output_map, input_map.T, precision=highest)
        by_head = cumulative.T
        spread = by_head[:, :, None] - by_head[:, None, :]
        decays = jnp.where(causal[None], jnp.exp(jnp.where(causal[None], spread, 0.0)), 0.0)
        mixing = scores[None] * decays * step_here.T[:, None, :]
        within = jnp.einsum('htr,rhp->thp', mixing, inner_x, precision=highest)
        across = jnp.exp(cumulative)[:, :, None] * jnp.einsum('tn,hpn->thp', output_map, entering, precision=highest)
        output = within + across + skip_gain[None, :, None] * inner_x
        weight_end = jnp.exp(cumulative[-1:] - cumulative) * step_here
        leaving = jnp.exp(cumulative[-1])[:, None, None] * entering + jnp.einsum('rh,rhp,rn->hpn', weight_end, inner_x, input_map, precision=highest)
        return (leaving, output)
    last_state, outputs = lax.scan(jax.checkpoint(group_step), jnp.zeros((HEADS, HEAD_DIM, STATE), jnp.float32), blocks)
    gated_out = outputs.reshape(length, INNER) * jax.nn.silu(gate_proj)
    normed = gated_out * lax.rsqrt(lax.optimization_barrier(jnp.mean(gated_out * gated_out, axis=-1, keepdims=True)) + epsilon) * out_gain
    return tokens + jnp.dot(normed, w_out, precision=highest)

def reference(tokens, norm_gain, w_gate, w_inner, w_state, w_step, conv_inner, conv_state, bias_inner, bias_state, step_bias, decay_log, skip_gain, out_gain, w_out, cotangent):
    weights_all = (norm_gain, w_gate, w_inner, w_state, w_step, conv_inner, conv_state, bias_inner, bias_state, step_bias, decay_log, skip_gain, out_gain, w_out)

    def per_sequence(running, seq_pair):
        seq_tokens, seq_cot = seq_pair
        out_seq, pullback = jax.vjp(mamba_layer, seq_tokens, *weights_all)
        gradients = pullback(seq_cot)
        running = tuple((acc + grad_one for acc, grad_one in zip(running, gradients[1:])))
        return (running, (out_seq, gradients[0]))
    zero_sums = tuple((jnp.zeros_like(weight_one) for weight_one in weights_all))
    grad_sums, (results, grad_tokens) = lax.scan(per_sequence, zero_sums, (tokens, cotangent))
    return (results, grad_tokens, grad_sums[0], grad_sums[1], grad_sums[2], grad_sums[3], grad_sums[4], grad_sums[5], grad_sums[6], grad_sums[7], grad_sums[8], grad_sums[9], grad_sums[10], grad_sums[11], grad_sums[12], grad_sums[13])
```

```python
import functools

import jax
import jax.numpy as jnp
from jax import lax
from jax.experimental import pallas as pl
from jax.experimental.pallas import tpu as pltpu
from jax.sharding import PartitionSpec as P

HEADS = 24
HEAD_DIM = 64
STATE = 128

highest = lax.Precision.HIGHEST
high = lax.Precision.HIGHEST
epsilon = 1e-05


def shifted(array, axis, by):
    length = lax.axis_size(axis)
    pairs = [(i, i + by) for i in range(length) if 0 <= i + by < length]
    return lax.ppermute(array, axis, pairs)


def scan_kernel(
    count, reverse, state_ref, decay_ref, out_ref,
    inbox, indecay, results, landed,
    send_a, recv_a, send_d, recv_d, send_b, recv_b,
):
    me = lax.axis_index("seq")
    barrier = pltpu.get_barrier_semaphore()

    def greet(d, carry):
        pl.semaphore_signal(
            barrier, inc=1, device_id={"seq": lax.rem(me + d, count)}, device_id_type=pl.DeviceIdType.MESH
        )
        return carry

    lax.fori_loop(1, count, greet, 0)
    pl.semaphore_wait(barrier, count - 1)

    def outward(d):
        to = lax.rem(me + d, count)
        return (
            pltpu.make_async_remote_copy(
                src_ref=state_ref.at[:, to], dst_ref=inbox.at[me], send_sem=send_a.at[d], recv_sem=recv_a.at[d],
                device_id={"seq": to}, device_id_type=pl.DeviceIdType.MESH,
            ),
            pltpu.make_async_remote_copy(
                src_ref=decay_ref, dst_ref=indecay.at[me], send_sem=send_d.at[d], recv_sem=recv_d.at[d],
                device_id={"seq": to}, device_id_type=pl.DeviceIdType.MESH,
            ),
        )

    def homeward(d):
        to = lax.rem(me + d, count)
        return pltpu.make_async_remote_copy(
            src_ref=results.at[to], dst_ref=landed.at[:, me], send_sem=send_b.at[d], recv_sem=recv_b.at[d],
            device_id={"seq": to}, device_id_type=pl.DeviceIdType.MESH,
        )

    def start_out(d, carry):
        for copy in outward(d):
            copy.start()
        return carry

    def wait_out(d, carry):
        for copy in outward(d):
            copy.wait()
        return carry

    def start_home(d, carry):
        homeward(d).start()
        return carry

    def wait_home(d, carry):
        homeward(d).wait()
        return carry

    lax.fori_loop(1, count, start_out, 0)
    inbox[pl.ds(me, 1)] = state_ref[:, pl.ds(me, 1)].reshape((1,) + inbox.shape[1:])
    indecay[pl.ds(me, 1)] = decay_ref[...][None]
    lax.fori_loop(1, count, wait_out, 0)

    for s in range(inbox.shape[1]):

        def hop(k, running):
            at = count - 1 - k if reverse else k
            results[at, s] = running
            return running * indecay[at, s : s + 1, :] + inbox[at, s]

        lax.fori_loop(0, count, hop, jnp.zeros(inbox.shape[2:], jnp.float32))
    lax.fori_loop(1, count, start_home, 0)
    landed[:, pl.ds(me, 1)] = results[pl.ds(me, 1)].reshape(
        (landed.shape[0], 1) + landed.shape[2:]
    )
    lax.fori_loop(1, count, wait_home, 0)
    out_ref[...] = landed[...]


def pass_states(state, decay, reverse):
    count = lax.axis_size("seq")
    seqs, depth, width = state.shape
    rows = depth // count
    parts = state.reshape(seqs, count, rows, width)
    spread = jnp.repeat(decay, HEAD_DIM, axis=-1)
    vmem = pl.BlockSpec(memory_space=pltpu.VMEM)
    boxes = (count, seqs, rows, width)
    sems = pltpu.SemaphoreType.DMA((count,))
    entering = pl.pallas_call(
        functools.partial(scan_kernel, count, reverse),
        out_shape=jax.ShapeDtypeStruct(parts.shape, jnp.float32),
        in_specs=[vmem, vmem],
        out_specs=vmem,
        scratch_shapes=[
            pltpu.VMEM(boxes, jnp.float32),
            pltpu.VMEM((count, seqs, width), jnp.float32),
            pltpu.VMEM(boxes, jnp.float32),
            pltpu.VMEM(parts.shape, jnp.float32),
            sems, sems, sems, sems, sems, sems,
        ],
        compiler_params=pltpu.CompilerParams(
            collective_id=1 if reverse else 0, has_side_effects=True, vmem_limit_bytes=40 * 2**20
        ),
        name="states_back" if reverse else "states_on",
    )(parts, spread)
    return entering.reshape(state.shape)


def product(left, right):
    return jnp.einsum("...k,kn->...n", left, right, precision=high)


def project(hidden, w_gate, w_inner, w_state, w_step):
    mixed_in = jnp.concatenate([product(hidden, w_inner), product(hidden, w_state)], axis=-1)
    return (product(hidden, w_gate), mixed_in, product(hidden, w_step))


def convolve(
    mixed_in, before, conv_inner, conv_state, bias_inner, bias_state, raw_step, step_bias, decay_log
):
    weights = jnp.concatenate([conv_inner, conv_state], axis=-1)
    summed = jnp.concatenate([bias_inner, bias_state], axis=-1) + jnp.zeros_like(mixed_in)
    padded = jnp.concatenate([before, mixed_in], axis=1)
    length = mixed_in.shape[1]
    for offset in range(weights.shape[0]):
        summed = summed + weights[offset] * padded[:, offset : offset + length]
    step_size = jax.nn.softplus(raw_step + step_bias)
    lower = jnp.tril(jnp.ones((length, length), jnp.float32))
    cumulative = jnp.einsum(
        "tr,srh->sth", lower, -jnp.exp(decay_log) * step_size, precision=highest
    )
    return (jax.nn.silu(summed), step_size, cumulative)


def unpack(active):
    inner_width = active.shape[-1] - 2 * STATE
    return (
        active[..., :inner_width],
        active[..., inner_width : inner_width + STATE],
        active[..., inner_width + STATE :],
    )


def by_channel(per_head):
    return jnp.repeat(per_head, HEAD_DIM, axis=-1)


def end_state(active, step_size, cumulative):
    inner_x, input_map, output_map = unpack(active)
    weight_end = jnp.exp(cumulative[:, -1:, :] - cumulative) * step_size
    local_state = jnp.einsum(
        "sln,slc->snc", input_map, inner_x * by_channel(weight_end), precision=highest
    )
    return (local_state, jnp.exp(cumulative[:, -1, :]))


def group_within(active, step_size, cumulative, skip_gain):
    inner_x, input_map, output_map = unpack(active)
    length = active.shape[1]
    scores = jnp.einsum("stn,srn->str", output_map, input_map, precision=high)
    by_head = jnp.transpose(cumulative, (0, 2, 1))
    causal = (jnp.arange(length)[:, None] >= jnp.arange(length)[None, :])[None, None]
    spread = by_head[:, :, :, None] - by_head[:, :, None, :]
    decays = jnp.where(causal, jnp.exp(jnp.where(causal, spread, 0.0)), 0.0)
    mixing = scores[:, None] * decays * jnp.transpose(step_size, (0, 2, 1))[:, :, None, :]
    heads = inner_x.reshape(inner_x.shape[:2] + (-1, HEAD_DIM))
    within = jnp.einsum("shtr,srhp->sthp", mixing, heads, precision=high)
    return within.reshape(inner_x.shape) + by_channel(skip_gain) * inner_x


def group_out(active, step_size, cumulative, entering, gate_proj, skip_gain):
    within = group_within(active, step_size, cumulative, skip_gain)
    output_map = unpack(active)[2]
    across = by_channel(jnp.exp(cumulative)) * jnp.einsum(
        "stn,snc->stc", output_map, entering, precision=highest
    )
    gated_out = (within + across) * jax.nn.silu(gate_proj)
    return (gated_out, jnp.sum(gated_out * gated_out, axis=-1))


def finish(gated_out, square_sum, out_gain, w_out):
    inverse = lax.rsqrt(square_sum / (HEADS * HEAD_DIM) + epsilon)
    return product(gated_out * inverse[..., None] * out_gain, w_out)


def after(array, earlier):
    return lax.optimization_barrier((array, earlier))


def body(
    tokens,
    norm_gain,
    w_gate,
    w_inner,
    w_state,
    w_step,
    conv_inner,
    conv_state,
    bias_inner,
    bias_state,
    step_bias,
    decay_log,
    skip_gain,
    out_gain,
    w_out,
    cotangent,
):
    width = tokens.shape[-1]
    full_cot = lax.all_gather(cotangent, "head", axis=2, tiled=True)
    inverse = lax.rsqrt(jnp.mean(tokens * tokens, axis=-1, keepdims=True) + epsilon)
    scaled = tokens * inverse
    hidden = scaled * norm_gain
    gate_proj, mixed_in, raw_step = project(hidden, w_gate, w_inner, w_state, w_step)
    edge_rows = conv_inner.shape[0] - 1
    before = shifted(mixed_in[:, mixed_in.shape[1] - edge_rows :], "seq", 1)
    (active, step_size, cumulative), convolve_back = jax.vjp(
        convolve,
        mixed_in,
        before,
        conv_inner,
        conv_state,
        bias_inner,
        bias_state,
        raw_step,
        step_bias,
        decay_log,
    )
    (local_state, decay_all), state_back = jax.vjp(end_state, active, step_size, cumulative)
    entering = pass_states(local_state, decay_all, False)
    (gated_out, partial_sq), group_back = jax.vjp(
        group_out, active, step_size, cumulative, entering, gate_proj, skip_gain
    )
    square_sum = lax.psum(partial_sq, "head")
    partial_out, finish_back = jax.vjp(finish, gated_out, square_sum, out_gain, w_out)
    shared_out = lax.psum_scatter(partial_out, "head", scatter_dimension=2, tiled=True)
    columns = shared_out.shape[2]
    col_start = lax.axis_index("head") * columns
    my_tokens = lax.dynamic_slice_in_dim(tokens, col_start, columns, 2)
    result = my_tokens + shared_out
    grad_gated, grad_square, grad_out_gain, grad_w_out = finish_back(full_cot)
    grad_partial_sq = lax.psum(grad_square, "head")
    grad_active, grad_step, grad_cumul, grad_entering, grad_gate, grad_skip_gain = group_back(
        (grad_gated, grad_partial_sq)
    )
    grad_w_gate = jnp.einsum("stk,stn->kn", hidden, grad_gate, precision=high)
    early = jnp.concatenate([grad_w_gate, grad_w_out], axis=0)
    grad_entering, early = after(grad_entering, early)
    sum_early = lax.psum(early, "seq")
    carried = pass_states(grad_entering, decay_all, True)
    grad_decay = jnp.sum(carried * entering, axis=1)
    grad_decay = jnp.sum(grad_decay.reshape(grad_decay.shape[0], -1, HEAD_DIM), axis=-1)
    more_active, more_step, more_cumul = state_back((carried, grad_decay))
    (
        grad_mixed,
        grad_before,
        grad_conv_inner,
        grad_conv_state,
        grad_bias_inner,
        grad_bias_state,
        grad_raw,
        grad_step_bias,
        grad_decay_log,
    ) = convolve_back((grad_active + more_active, grad_step + more_step, grad_cumul + more_cumul))
    returned = shifted(grad_before, "seq", -1)
    grad_mixed = grad_mixed.at[:, grad_mixed.shape[1] - edge_rows :].add(returned)
    grad_inner = grad_mixed[..., : w_inner.shape[1]]
    grad_maps = grad_mixed[..., w_inner.shape[1] :]
    grad_w_inner = jnp.einsum("stk,stn->kn", hidden, grad_inner, precision=high)
    grad_maps_t = jnp.einsum("stn,stk->nk", grad_maps, hidden, precision=high)
    grad_step_t = jnp.einsum("stn,stk->nk", grad_raw, hidden, precision=high)
    grad_hidden = (
        jnp.einsum("stn,kn->stk", grad_gate, w_gate, precision=high)
        + jnp.einsum("stn,kn->stk", grad_inner, w_inner, precision=high)
        + jnp.einsum("stn,kn->stk", grad_maps, w_state, precision=high)
        + jnp.einsum("stn,kn->stk", grad_raw, w_step, precision=high)
    )

    maps = w_state.shape[1]
    taps = conv_state.shape[0]
    loose = jnp.concatenate([grad_conv_state.reshape(-1), grad_bias_state])
    loose_rows = -(-loose.size // width)
    shared_rows = maps + 1 + loose_rows
    fill = -shared_rows % 16
    shared = jnp.concatenate(
        [
            grad_maps_t,
            jnp.sum(grad_hidden * scaled, axis=(0, 1))[None],
            jnp.pad(loose, (0, loose_rows * width - loose.size)).reshape(loose_rows, width),
            jnp.zeros((fill, width), jnp.float32),
        ],
        axis=0,
    )
    shared = lax.psum_scatter(shared, "head", scatter_dimension=0, tiled=True)
    small = jnp.concatenate([grad_step_bias, grad_decay_log, grad_skip_gain])
    heads = step_bias.shape[0]
    channels = w_inner.shape[1]
    packed = jnp.concatenate(
        [
            grad_conv_inner,
            grad_bias_inner[None],
            grad_out_gain[None],
            jnp.pad(small, (0, channels - small.size))[None],
        ],
        axis=0,
    )
    packed = jnp.concatenate([grad_w_inner, shared, grad_step_t, packed], axis=0)
    packed, sum_early = after(packed, sum_early)
    total = lax.psum(packed, "seq")

    my_hidden = lax.psum_scatter(grad_hidden, "head", scatter_dimension=2, tiled=True)
    along = lax.psum(jnp.sum(grad_hidden * hidden, axis=-1), "head")[..., None]
    my_gain = lax.dynamic_slice_in_dim(norm_gain, col_start, columns, 0)
    grad_tokens = (
        cotangent + inverse * my_gain * my_hidden - my_tokens * (inverse * inverse * along / width)
    )

    at = 0

    def take(rows):
        nonlocal at
        at += rows
        return total[at - rows : at]

    sum_w_inner = take(width)
    sum_shared = lax.all_gather(take(shared.shape[0]), "head", axis=0, tiled=True)
    sum_w_step = take(heads).T
    sum_conv_inner = take(taps)
    sum_bias_inner = take(1)[0]
    sum_out_gain = take(1)[0]
    sums = take(1)[0]
    loose = sum_shared[maps + 1 : shared_rows].reshape(-1)
    sum_conv_state = loose[: taps * maps].reshape(taps, maps)
    sum_bias_state = loose[taps * maps : (taps + 1) * maps]
    return (
        result,
        grad_tokens,
        sum_shared[maps],
        sum_early[:width],
        sum_w_inner,
        sum_shared[:maps].T,
        sum_w_step,
        sum_conv_inner,
        sum_conv_state,
        sum_bias_inner,
        sum_bias_state,
        sums[:heads],
        sums[heads : 2 * heads],
        sums[2 * heads : 3 * heads],
        sum_out_gain,
        sum_early[width:],
    )


def solution(mesh):
    return jax.shard_map(
        body,
        mesh=mesh,
        in_specs=(
            P(None, "seq", None),
            P(),
            P(None, "head"),
            P(None, "head"),
            P(),
            P(None, "head"),
            P(None, "head"),
            P(),
            P("head"),
            P(),
            P("head"),
            P("head"),
            P("head"),
            P("head"),
            P("head", None),
            P(None, "seq", "head"),
        ),
        out_specs=(
            P(None, "seq", "head"),
            P(None, "seq", "head"),
            P(),
            P(None, "head"),
            P(None, "head"),
            P(),
            P(None, "head"),
            P(None, "head"),
            P(),
            P("head"),
            P(),
            P("head"),
            P("head"),
            P("head"),
            P("head"),
            P("head", None),
        ),
        check_vma=False,
    )
```
